256 devices in a mesh: row: 16 (over y, z_hi, core), col: 16 (over x, z_lo).
Axes of the slice: x: 4, y: 4, z: 8 (z_hi: 2, z_lo: 4; z = z_hi * 4 + z_lo), core: 2. Of those that a mesh axis runs over, the one named last changes fastest.
Arguments:
- p_blocks: bfloat16 [16, 16, 32, 128, 128], P('row', 'col')
- coords: int32 [16, 16, 2, 32], P('row', 'col'), may hold values from 0 to 2047, as said below
- tasks: int32 [16, 16, 4, 3, 256], P('row', 'col'), may hold values from -1 to 31, as said below
- window_panels: int32 [4], replicated, may hold values from 0 to 31, as said below
- branch: int32 [16, 16, 32], P('row', 'col'), may hold values from 0 to 1
Outputs:
- p_next: bfloat16 [16, 16, 32, 128, 128], P('row', 'col')
- traces: float32 [2], replicated
The draws below stay inside these ranges and needn't reach their ends.
Inputs may be any that keep to these rules, and one draw needn't show every extreme that they name: `coords`: global block row and column lie in the block's row and column panel; in each pair of equal row and column panels exactly 4 of the 8 slots are diagonal blocks, no other block is. `tasks`: index 0 is below 32 or -1, index 1 below 16, index 2 below 16; in each device's step the live products come first, 128 or more of them, and all 256 are live in some device's step. `window_panels`: distinct panel numbers; the last panel is among them.
All inputs are finite; a program needn't handle non-finite values.
Results may differ from the reference program's by a relative error of at most 0.001.
Values may be sent and summed in bfloat16 or wider, within the bound.
No kernel may reach another device: no remote copies, remote signals or barrier semaphores. Data moves between devices by JAX's collectives and lax.ppermute only.
A program may use at most 64 MiB of HBM per device.

```python
import jax
import jax.numpy as jnp
from jax import lax

BS = 128
PB = 64
WIN = 4
Q = 8
M = 256
NPAN = 32
PANR = 2
PANC = 2
NO = 32
NA = 16
NB = 16
N_ROW = 16
N_COL = 16


def draw_p_blocks(key, part):
    key = jax.random.fold_in(key, 11)
    first, second = jax.random.split(key)
    shape = (N_ROW, N_COL, NO, BS, BS)
    noise = jax.random.normal(first, shape, jnp.float32)
    spread = 0.5
    exponent = jax.random.uniform(second, (N_ROW, N_COL, NO, BS, 1), jnp.float32, -spread, spread)
    row_scale = jnp.power(10.0, exponent)
    rise = 1.0 + 2.0 * jnp.arange(N_ROW, dtype=jnp.float32) / max(N_ROW - 1, 1)
    rise = rise.reshape(N_ROW, 1, 1, 1, 1)
    eye = jnp.eye(BS, dtype=jnp.float32)
    values = (noise * row_scale * BS ** (-0.25) + 0.5 * eye) * rise
    return values.astype(jnp.bfloat16)


def draw_coords(key, part):
    key = jax.random.fold_in(key, 12)
    first, second, third, fourth = jax.random.split(key, 4)
    slot = jnp.arange(NO, dtype=jnp.int32)
    inner_i = slot // (PANC * Q)
    inner_j = slot // Q % PANC
    grid_rows = jnp.arange(N_ROW, dtype=jnp.int32).reshape(N_ROW, 1, 1)
    grid_cols = jnp.arange(N_COL, dtype=jnp.int32).reshape(1, N_COL, 1)
    row_panel = grid_rows * PANR + inner_i.reshape(1, 1, NO)
    col_panel = grid_cols * PANC + inner_j.reshape(1, 1, NO)
    row_panel = jnp.broadcast_to(row_panel, (N_ROW, N_COL, NO))
    col_panel = jnp.broadcast_to(col_panel, (N_ROW, N_COL, NO))
    row_inner = jax.random.randint(first, (N_ROW, N_COL, NO), 0, PB)
    col_inner = jax.random.randint(second, (N_ROW, N_COL, NO), 0, PB)
    offset = jax.random.randint(third, (N_ROW, N_COL, NO), 0, max(PB - 1, 1)) + 1
    same_panel = row_panel == col_panel
    col_inner = jnp.where(same_panel, (row_inner + offset) % PB, col_inner)
    scores = jax.random.randint(fourth, (N_ROW, N_COL, PANR * PANC, Q), 0, 1 << 20)
    scores = scores * Q + jnp.arange(Q, dtype=jnp.int32).reshape(1, 1, 1, Q)
    order = jnp.argsort(scores, axis=-1)
    ranks = jnp.argsort(order, axis=-1).reshape(N_ROW, N_COL, NO)
    diagonal = same_panel & (ranks < Q // 2)
    col_inner = jnp.where(diagonal, row_inner, col_inner)
    rows_global = row_panel * PB + row_inner
    cols_global = col_panel * PB + col_inner
    return jnp.stack([rows_global, cols_global], axis=2).astype(jnp.int32)


def draw_tasks(key, part):
    key = jax.random.fold_in(key, 13)
    keys = jax.random.split(key, 5)
    counts = jax.random.randint(keys[0], (N_ROW, N_COL, WIN), M // 2, M + 1)
    chosen = jax.random.randint(keys[1], (), 0, N_ROW * N_COL * WIN)
    flat_pos = jnp.arange(N_ROW * N_COL * WIN, dtype=jnp.int32).reshape(N_ROW, N_COL, WIN)
    counts = jnp.where(flat_pos == chosen, M, counts)
    outputs = jax.random.randint(keys[2], (N_ROW, N_COL, WIN, M), 0, NO)
    live = jnp.arange(M, dtype=jnp.int32).reshape(1, 1, 1, M) < counts[..., None]
    outputs = jnp.where(live, outputs, -1)
    left_ids = jax.random.randint(keys[3], (N_ROW, N_COL, WIN, M), 0, NA)
    right_ids = jax.random.randint(keys[4], (N_ROW, N_COL, WIN, M), 0, NB)
    return jnp.stack([outputs, left_ids, right_ids], axis=3).astype(jnp.int32)


def draw_window_panels(key, part):
    key = jax.random.fold_in(key, 14)
    first, second = jax.random.split(key)
    others = jax.random.permutation(first, NPAN - 1)[:WIN - 1]
    chosen = jnp.concatenate([others, jnp.array([NPAN - 1])]).astype(jnp.int32)
    return jax.random.permutation(second, chosen).astype(jnp.int32)


def plant(entries, key, least, high):
    place = [jax.random.randint(jax.random.fold_in(key, axis), (), 0, length) for axis, length in enumerate(entries.shape)]
    longest = entries.shape.index(max(entries.shape))
    beside = place[:longest] + [(place[longest] + 1) % entries.shape[longest]] + place[longest + 1:]
    return entries.at[tuple(place)].set(least).at[tuple(beside)].set(high)


def setup_inputs(seed: int = 0) -> dict:
    key_list = jax.random.split(jax.random.key(seed), 6)
    p_blocks = draw_p_blocks(jax.random.fold_in(key_list[5], 71), 0)
    coords = draw_coords(jax.random.fold_in(key_list[5], 71), 0)
    tasks = draw_tasks(jax.random.fold_in(key_list[5], 71), 0)
    window_panels = draw_window_panels(jax.random.fold_in(key_list[5], 71), 0)
    branch = plant(jax.random.randint(key_list[4], (N_ROW, N_COL, NO), 0, 2), jax.random.fold_in(key_list[4], 1), 0, 1).astype(jnp.int32)
    return {"p_blocks": p_blocks, "coords": coords, "tasks": tasks, "window_panels": window_panels, "branch": branch}


def block_trace(blocks):
    return jnp.sum(jnp.diagonal(blocks, axis1=1, axis2=2), axis=-1)


def reference(p_blocks, coords, tasks, window_panels, branch):
    tiles_all = p_blocks.reshape(N_ROW, N_COL, PANR, PANC, Q, BS, BS)

    def device_work(flat):
        grid_row = flat // N_COL
        grid_col = flat % N_COL
        product = jnp.zeros((NO, BS, BS), jnp.float32)
        for step in range(WIN):
            panel = window_panels[step]
            col_tiles = tiles_all[grid_row, panel // PANC]
            col_panel = col_tiles[:, panel % PANC].reshape(NA, BS, BS)
            row_tiles = tiles_all[panel // PANR, grid_col]
            row_panel = row_tiles[panel % PANR].reshape(NB, BS, BS)
            step_tasks = tasks[grid_row, grid_col, step]
            left_blocks = col_panel[step_tasks[1]].astype(jnp.float32)
            right_blocks = row_panel[step_tasks[2]].astype(jnp.float32)
            prods = jnp.einsum("tij,tjk->tik", left_blocks, right_blocks, precision=lax.Precision.HIGHEST)
            target = jnp.where(step_tasks[0] < 0, NO, step_tasks[0]).astype(jnp.int32)
            product = product + jax.ops.segment_sum(prods, target, num_segments=NO + 1)[:NO]
        own_blocks = p_blocks[grid_row, grid_col].astype(jnp.float32)
        own_branch = branch[grid_row, grid_col].reshape(NO, 1, 1)
        purified = jnp.where(own_branch == 0, product, 2.0 * own_blocks - product)
        diag_mask = (coords[grid_row, grid_col, 0] == coords[grid_row, grid_col, 1]).astype(jnp.float32)
        old_part = jnp.sum(diag_mask * block_trace(own_blocks))
        new_part = jnp.sum(diag_mask * block_trace(purified))
        return purified.astype(jnp.bfloat16), old_part, new_part

    flat_ids = jnp.arange(N_ROW * N_COL, dtype=jnp.int32)
    next_blocks, old_parts, new_parts = lax.map(device_work, flat_ids)
    scale_factor = 1.0 / (NPAN * (Q // 2) * BS) ** 0.5
    traces = jnp.stack([jnp.sum(old_parts), jnp.sum(new_parts)]) * scale_factor
    return next_blocks.reshape(N_ROW, N_COL, NO, BS, BS), traces.astype(jnp.float32)
```

```python
import functools

import jax
import jax.numpy as jnp
from jax import lax
from jax.experimental import pallas as pl
from jax.experimental.pallas import tpu as pltpu
from jax.sharding import PartitionSpec as P

BS = 128
Q = 8
WIN = 4
NO = 32
TASKS = 1024
GROUP = 4
UNROLL = 4
NGROUP = 288
ZERO = 64
SCALE = 1.0 / (32 * 4 * 128) ** 0.5


def swap(value, axis, bit):
    return lax.ppermute(value, axis, [(i, i ^ bit) for i in range(16)])


def pick(stack, index):
    return lax.dynamic_index_in_dim(stack, index, 0, keepdims=False)


def column_panels(tiles, panels):
    me = lax.axis_index("col")
    x, z = me // 4, me % 4
    by_x = jnp.moveaxis(tiles, 2, 0)
    parts = [pick(by_x, x)] + [swap(pick(by_x, x ^ d), "col", 4 * d) for d in (1, 2, 3)]
    parts = jnp.moveaxis(jnp.stack(parts), 2, 1).reshape(8, 4, BS, BS)
    owner = panels // 2
    mine = [pick(parts, (x ^ (owner[s] // 4)) * 2 + panels[s] % 2) for s in range(WIN)]
    by_z = jnp.stack(mine, 1)
    parts = [pick(by_z, z)] + [swap(pick(by_z, z ^ d), "col", d) for d in (1, 2, 3)]
    parts = jnp.stack(parts)
    held = jnp.stack([pick(parts[:, s], z ^ (owner[s] % 4)) for s in range(WIN)])
    line = jnp.concatenate([held] + [swap(held, "col", d) for d in (1, 2, 3)])
    return [line] + [swap(line, "col", 4 * d) for d in (1, 2, 3)]


def row_panels(tiles, panels):
    me = lax.axis_index("row")
    y, zh, core = me // 4, (me // 2) % 2, me % 2
    by_y = jnp.moveaxis(tiles, 2, 0)
    parts = [pick(by_y, y)] + [swap(pick(by_y, y ^ d), "row", 4 * d) for d in (1, 2, 3)]
    parts = jnp.stack(parts).reshape(8, 2, 2, BS, BS)
    owner = panels // 2
    mine = [pick(parts, (y ^ (owner[s] // 4)) * 2 + panels[s] % 2) for s in range(WIN)]
    by_j = jnp.stack(mine, 1)
    own = pick(by_j, core)
    got = swap(pick(by_j, 1 - core), "row", 1)
    here = (owner % 2 == core).reshape(WIN, 1, 1, 1)
    half = jnp.where(here, own, got)
    got = swap(half, "row", 2)
    here = ((owner // 2) % 2 == zh).reshape(WIN, 1, 1, 1)
    half = jnp.where(here, half, got).reshape(WIN * 2, BS, BS)
    line = jnp.concatenate([half] + [swap(half, "row", 4 * d) for d in (1, 2, 3)])
    return [line, swap(line, "row", 1)]


def plan(tasks, coords):
    me_r, me_c = lax.axis_index("row"), lax.axis_index("col")
    x, z = me_c // 4, me_c % 4
    y, core = me_r // 4, me_r % 2
    outs = tasks[:, 0].reshape(TASKS)
    left = tasks[:, 1].reshape(TASKS)
    right = tasks[:, 2].reshape(TASKS)
    step = jnp.arange(TASKS, dtype=jnp.int32) // (TASKS // WIN)
    left = (x ^ (left % 8 // 2)) * 16 + (z ^ (left // 8 * 2 + left % 2)) * 4 + step
    right = (core ^ (right // 8)) * 32 + (y ^ (right % 8 // 2)) * 8 + step * 2 + right % 2
    slots = jnp.arange(NO, dtype=jnp.int32)
    hot = outs[:, None] == slots[None, :]
    hot_bf = hot.astype(jnp.bfloat16)
    ids = jnp.arange(TASKS, dtype=jnp.int32)
    earlier = (ids[None, :] < ids[:, None]).astype(jnp.bfloat16)
    seen = jnp.dot(earlier, hot_bf, preferred_element_type=jnp.float32).astype(jnp.int32)
    counts = jnp.sum(hot.astype(jnp.int32), axis=0)
    groups = (counts + GROUP - 1) // GROUP
    diag = coords[0] == coords[1]
    order = jnp.where(diag, 0, NO) + slots
    starts = jnp.sum(jnp.where(order[None, :] < order[:, None], groups[None, :], 0), axis=1)
    place = jnp.sum(jnp.where(hot, seen + GROUP * starts[None, :], 0), axis=1)
    place = jnp.where(outs >= 0, place, -1)
    spots = jnp.arange(NGROUP * GROUP, dtype=jnp.int32)
    move = (spots[:, None] == place[None, :]).astype(jnp.bfloat16)
    pair = jnp.stack([left - ZERO, right], axis=1).astype(jnp.bfloat16)
    lists = jnp.dot(move, pair, preferred_element_type=jnp.float32).astype(jnp.int32)
    gid = jnp.arange(NGROUP, dtype=jnp.int32)[:, None]
    inside = (gid >= starts[None, :]) & (gid < (starts + groups)[None, :])
    target = jnp.sum(jnp.where(inside, slots[None, :], 0), axis=1)
    total = jnp.sum(groups)
    diag_total = jnp.sum(jnp.where(diag, groups, 0))
    return lists[:, 0] + ZERO, lists[:, 1], target, jnp.stack([total, diag_total]), diag.astype(jnp.int32)


def group_product(left_ref, right_ref, lhs, rhs, group):
    spots = [group * GROUP + k for k in range(GROUP)]
    a = jnp.concatenate([lhs[left_ref[t]] for t in spots], axis=1)
    b = jnp.concatenate([rhs[right_ref[t]] for t in spots], axis=0)
    return jnp.dot(a, b, preferred_element_type=jnp.float32)


def trace_kernel(left_ref, right_ref, target_ref, total_ref, branch_ref, diag_ref, lhs, rhs, own, out, old, new):
    out[...] = jnp.zeros_like(out)
    any_diag = functools.reduce(jnp.maximum, [diag_ref[o] for o in range(NO)])

    @pl.when(any_diag > 0)
    def _():
        old[...] = jnp.zeros_like(old)
        new[...] = jnp.zeros_like(new)

        def add_own(o, carry):
            @pl.when(diag_ref[o] > 0)
            def _():
                block = own[o].astype(jnp.float32)
                old[...] += block
                new[...] += block * jnp.where(branch_ref[o] == 0, 0.0, 2.0)

            return carry

        lax.fori_loop(0, NO, add_own, 0)

        def one(g, carry):
            part = group_product(left_ref, right_ref, lhs, rhs, g)
            new[...] += part * jnp.where(branch_ref[target_ref[g]] == 0, 1.0, -1.0)
            return carry

        lax.fori_loop(0, total_ref[1], one, 0)
        shape = (BS, BS)
        eye = lax.broadcasted_iota(jnp.int32, shape, 0) == lax.broadcasted_iota(jnp.int32, shape, 1)
        out[0:1, :] = jnp.sum(jnp.where(eye, old[...], 0.0), axis=0, keepdims=True)
        out[1:2, :] = jnp.sum(jnp.where(eye, new[...], 0.0), axis=0, keepdims=True)


def main_kernel(left_ref, right_ref, target_ref, total_ref, branch_ref, lhs, rhs, own, out, acc):
    acc[...] = jnp.zeros_like(acc)

    def some(it, carry):
        for u in range(UNROLL):
            g = it * UNROLL + u
            part = group_product(left_ref, right_ref, lhs, rhs, g)
            o = target_ref[g]
            acc[o] += part
        return carry

    lax.fori_loop(0, (total_ref[0] + UNROLL - 1) // UNROLL, some, 0)

    def finish(o, carry):
        product = acc[o]
        flip = 2.0 * own[o].astype(jnp.float32) - product
        out[o] = jnp.where(branch_ref[o] == 0, product, flip).astype(jnp.bfloat16)
        return carry

    lax.fori_loop(0, NO, finish, 0)


def reduce_all(value):
    for axis, bits in (("row", (1, 2)), ("row", (4, 8)), ("col", (1, 2)), ("col", (4, 8))):
        low, high = bits
        one, two, three = (swap(value, axis, b) for b in (low, high, low + high))
        value = (value + one) + (two + three)
    return value


def body(p_blocks, coords, tasks, window_panels, branch):
    own = p_blocks[0, 0]
    tiles = own.reshape(2, 2, 4, 2, BS, BS)
    left, right, target, totals, diag = plan(tasks[0, 0], coords[0, 0])
    columns = column_panels(tiles, window_panels)
    rows = row_panels(tiles, window_panels)
    lhs = jnp.concatenate(columns + [jnp.zeros((1, BS, BS), jnp.bfloat16)])
    rhs = jnp.concatenate(rows)
    smem = pl.BlockSpec(memory_space=pltpu.SMEM)
    vmem = pl.BlockSpec(memory_space=pltpu.VMEM)
    params = pltpu.CompilerParams(vmem_limit_bytes=24 << 20)
    part = pl.pallas_call(
        trace_kernel,
        out_shape=jax.ShapeDtypeStruct((8, BS), jnp.float32),
        in_specs=[smem] * 6 + [vmem] * 3,
        out_specs=vmem,
        scratch_shapes=[pltpu.VMEM((BS, BS), jnp.float32)] * 2,
        compiler_params=params,
        name="trace_part",
    )(left, right, target, totals, branch[0, 0], diag, lhs, rhs, own)
    traces = jnp.sum(reduce_all(part), axis=1)[:2] * SCALE
    p_next = pl.pallas_call(
        main_kernel,
        out_shape=jax.ShapeDtypeStruct((NO, BS, BS), jnp.bfloat16),
        in_specs=[smem] * 5 + [vmem] * 3,
        out_specs=vmem,
        scratch_shapes=[pltpu.VMEM((NO, BS, BS), jnp.float32)],
        compiler_params=params,
        cost_estimate=pl.CostEstimate(flops=4 << 30, bytes_accessed=8 << 20, transcendentals=0),
        name="block_products",
    )(left, right, target, totals, branch[0, 0], lhs, rhs, own)
    return p_next[None, None], traces


def solution(mesh):
    in_specs = (
        P("row", "col", None, None, None),
        P("row", "col", None, None),
        P("row", "col", None, None, None),
        P(),
        P("row", "col", None),
    )
    out_specs = (P("row", "col", None, None, None), P())
    return jax.shard_map(body, mesh=mesh, in_specs=in_specs, out_specs=out_specs, check_vma=False)
```

```python
import functools

import jax
import jax.numpy as jnp
from jax import lax
from jax.experimental import pallas as pl
from jax.experimental.pallas import tpu as pltpu
from jax.sharding import PartitionSpec as P

BS = 128
WIN = 4
NO = 32
TASKS = 1024
GROUP = 4
UNROLL = 8
NGROUP = 288
ZERO = 64
FIRST = 8
SCALE = 1.0 / (32 * 4 * 128) ** 0.5


def swap(value, axis, bit):
    return lax.ppermute(value, axis, [(i, i ^ bit) for i in range(16)])


def pick(stack, index):
    return lax.dynamic_index_in_dim(stack, index, 0, keepdims=False)


def choose(parts, index):
    mask_shape = (WIN,) + (1,) * (parts[0].ndim - 1)
    out = jnp.broadcast_to(parts[0], (WIN,) + parts[0].shape[1:])
    for d in range(1, len(parts)):
        out = jnp.where((index == d).reshape(mask_shape), parts[d], out)
    return out


def scatter_columns(by_x, panels, x):
    parts = [pick(by_x, x)] + [swap(pick(by_x, x ^ d), "col", 4 * d) for d in (1, 2, 3)]
    index = ((x ^ (panels >> 3)) << 1) | (panels & 1)
    return choose([part[None, :, j] for part in parts for j in range(2)], index)


def scatter_rows(by_y, panels, y):
    parts = [pick(by_y, y)] + [swap(pick(by_y, y ^ d), "row", 4 * d) for d in (1, 2, 3)]
    index = ((y ^ (panels >> 3)) << 1) | (panels & 1)
    return choose([part[None, i] for part in parts for i in range(2)], index)


def panels_to_all(own, panels):
    me_r, me_c = lax.axis_index("row"), lax.axis_index("col")
    x, z = me_c >> 2, me_c & 3
    y, zh, core = me_r >> 2, (me_r >> 1) & 1, me_r & 1
    by_q = jnp.moveaxis(own.reshape(2, 2, 4, 2, BS, BS), 2, 0)
    mine = scatter_columns(by_q, panels, x).reshape(WIN, 4, BS, BS)
    by_j = scatter_rows(by_q, panels, y)

    by_z = jnp.moveaxis(mine, 1, 0)
    parts = [pick(by_z, z)] + [swap(pick(by_z, z ^ d), "col", d) for d in (1, 2, 3)]
    held = choose(parts, z ^ ((panels >> 1) & 3))

    by_j = jnp.moveaxis(by_j, 1, 0)
    got = swap(pick(by_j, 1 - core), "row", 1)
    half = choose([pick(by_j, core), got], ((panels >> 1) & 1) ^ core)

    line = jnp.concatenate([held] + [swap(held, "col", d) for d in (1, 2, 3)])
    line, half = lax.optimization_barrier((line, half))
    columns = [line] + [swap(line, "col", 4 * d) for d in (1, 2, 3)]

    half = choose([half, swap(half, "row", 2)], ((panels >> 2) & 1) ^ zh).reshape(WIN * 2, BS, BS)
    half, columns[1], columns[3] = lax.optimization_barrier((half, columns[1], columns[3]))
    line = jnp.concatenate([half] + [swap(half, "row", 4 * d) for d in (1, 2, 3)])
    return columns, [line, swap(line, "row", 1)]


def plan(tasks, coords):
    me_r, me_c = lax.axis_index("row"), lax.axis_index("col")
    x, z = me_c >> 2, me_c & 3
    y, core = me_r >> 2, me_r & 1
    outs = tasks[:, 0].reshape(TASKS)
    left = tasks[:, 1].reshape(TASKS)
    right = tasks[:, 2].reshape(TASKS)
    step = jnp.arange(TASKS, dtype=jnp.int32) >> 8
    left = ((x ^ ((left & 7) >> 1)) << 4) + ((z ^ (((left >> 3) << 1) + (left & 1))) << 2) + step
    right = ((core ^ (right >> 3)) << 5) + ((y ^ ((right & 7) >> 1)) << 3) + (step << 1) + (right & 1)
    slots = jnp.arange(NO, dtype=jnp.int32)
    hot = outs[:, None] == slots[None, :]
    hot_bf = hot.astype(jnp.bfloat16)
    ids = jnp.arange(TASKS, dtype=jnp.int32)
    earlier = (ids[None, :] < ids[:, None]).astype(jnp.bfloat16)
    seen = jnp.dot(earlier, hot_bf, preferred_element_type=jnp.float32).astype(jnp.int32)
    counts = jnp.sum(hot.astype(jnp.int32), axis=0)
    groups = (counts + GROUP - 1) >> 2
    diag = coords[0] == coords[1]
    order = jnp.where(diag, 0, NO) + slots
    before = order[None, :] < order[:, None]
    starts = jnp.sum(jnp.where(before, groups[None, :], 0), axis=1)
    rank = jnp.sum(before.astype(jnp.int32), axis=1)
    place = jnp.sum(jnp.where(hot, seen + GROUP * starts[None, :], 0), axis=1)
    place = jnp.where(outs >= 0, place, -1)
    spots = jnp.arange(NGROUP * GROUP, dtype=jnp.int32)
    move = (spots[:, None] == place[None, :]).astype(jnp.bfloat16)
    pair = jnp.stack([left - ZERO, right], axis=1).astype(jnp.bfloat16)
    lists = jnp.dot(move, pair, preferred_element_type=jnp.float32).astype(jnp.int32)
    gid = jnp.arange(NGROUP, dtype=jnp.int32)[:, None]
    target = jnp.sum((gid >= (starts + groups)[None, :]).astype(jnp.int32), axis=1)
    slot_of = jnp.sum(jnp.where(rank[:, None] == slots[None, :], slots[:, None], 0), axis=0)
    limits = jnp.array([0, FIRST, NO], jnp.int32)
    bounds = jnp.sum(jnp.where(rank[None, :] < limits[:, None], groups[None, :], 0), axis=1)
    return lists[:, 0] + ZERO, lists[:, 1], target, bounds, slot_of, diag.astype(jnp.int32)


def group_product(left_ref, right_ref, lhs, rhs, group):
    spots = [group * GROUP + k for k in range(GROUP)]
    a = jnp.concatenate([lhs[left_ref[t]] for t in spots], axis=1)
    b = jnp.concatenate([rhs[right_ref[t]] for t in spots], axis=0)
    return jnp.dot(a, b, preferred_element_type=jnp.float32)


def accumulate(part, base, count, left_ref, right_ref, target_ref, bounds_ref, lhs, rhs, acc):
    acc[...] = jnp.zeros_like(acc)
    first, last = bounds_ref[part], bounds_ref[part + 1]

    def some(it, carry):
        for u in range(UNROLL):
            g = first + it * UNROLL + u
            product = group_product(left_ref, right_ref, lhs, rhs, g)
            acc[jnp.minimum(target_ref[g] - base, count)] += product
        return carry

    lax.fori_loop(0, (last - first + UNROLL - 1) >> 3, some, 0)


def first_kernel(left_ref, right_ref, target_ref, bounds_ref, slot_ref, branch_ref, diag_ref, lhs, rhs, own, out, sums, acc, old, new):
    old[...] = jnp.zeros_like(old)
    new[...] = jnp.zeros_like(new)
    accumulate(0, 0, FIRST, left_ref, right_ref, target_ref, bounds_ref, lhs, rhs, acc)

    def finish(i, carry):
        o = slot_ref[i]
        product = acc[i]
        block = own[o].astype(jnp.float32)
        value = jnp.where(branch_ref[o] == 0, product, 2.0 * block - product)
        out[i] = value.astype(jnp.bfloat16)

        @pl.when(diag_ref[o] > 0)
        def _():
            old[...] += block
            new[...] += value

        return carry

    lax.fori_loop(0, FIRST, finish, 0)
    shape = (BS, BS)
    eye = lax.broadcasted_iota(jnp.int32, shape, 0) == lax.broadcasted_iota(jnp.int32, shape, 1)
    sums[...] = jnp.zeros_like(sums)
    sums[0:1, :] = jnp.sum(jnp.where(eye, old[...], 0.0), axis=0, keepdims=True)
    sums[1:2, :] = jnp.sum(jnp.where(eye, new[...], 0.0), axis=0, keepdims=True)


def rest_kernel(left_ref, right_ref, target_ref, bounds_ref, slot_ref, branch_ref, diag_ref, lhs, rhs, own, filled, out, acc):
    accumulate(1, FIRST, NO - FIRST, left_ref, right_ref, target_ref, bounds_ref, lhs, rhs, acc)

    def copy(i, carry):
        out[slot_ref[i]] = filled[i]
        return carry

    lax.fori_loop(0, FIRST, copy, 0)

    def finish(i, carry):
        o = slot_ref[FIRST + i]
        product = acc[i]
        value = jnp.where(branch_ref[o] == 0, product, 2.0 * own[o].astype(jnp.float32) - product)
        out[o] = value.astype(jnp.bfloat16)
        return carry

    lax.fori_loop(0, NO - FIRST, finish, 0)


def products(kernel, count, out_shape, scratch, scalars, arrays):
    smem = pl.BlockSpec(memory_space=pltpu.SMEM)
    vmem = pl.BlockSpec(memory_space=pltpu.VMEM)
    return pl.pallas_call(
        kernel,
        out_shape=out_shape,
        in_specs=[smem] * len(scalars) + [vmem] * len(arrays),
        out_specs=jax.tree.map(lambda _: vmem, out_shape),
        scratch_shapes=[pltpu.VMEM((n, BS, BS) if n else (BS, BS), jnp.float32) for n in scratch],
        compiler_params=pltpu.CompilerParams(vmem_limit_bytes=16 << 20),
        cost_estimate=pl.CostEstimate(flops=count << 27, bytes_accessed=8 << 20, transcendentals=0),
        name="block_products",
    )(*scalars, *arrays)


def body(p_blocks, coords, tasks, window_panels, branch):
    own = p_blocks[0, 0]
    left, right, target, bounds, slot_of, diag = plan(tasks[0, 0], coords[0, 0])
    columns, rows = panels_to_all(own, window_panels)
    lhs = jnp.concatenate(columns + [jnp.zeros((1, BS, BS), jnp.bfloat16)])
    arrays = (lhs, jnp.concatenate(rows), own)
    scalars = (left, right, target, bounds, slot_of, branch[0, 0], diag)
    shapes = (jax.ShapeDtypeStruct((FIRST, BS, BS), jnp.bfloat16), jax.ShapeDtypeStruct((8, BS), jnp.float32))
    filled, value = products(first_kernel, FIRST, shapes, (FIRST + 1, 0, 0), scalars, arrays)
    for axis, low, high in (("row", 1, 2), ("row", 4, 8), ("col", 1, 2)):
        one, two, three = (swap(value, axis, b) for b in (low, high, low + high))
        value = (value + one) + (two + three)
    value, filled = lax.optimization_barrier((value, filled))
    one, two, three = (swap(value, "col", b) for b in (4, 8, 12))
    shapes = jax.ShapeDtypeStruct((NO, BS, BS), jnp.bfloat16)
    out = products(rest_kernel, NO - FIRST, shapes, (NO - FIRST + 1,), scalars, arrays + (filled,))
    value = (value + one) + (two + three)
    traces = jnp.sum(value, axis=1)[:2] * SCALE
    return out[None, None], traces


def solution(mesh):
    in_specs = (
        P("row", "col", None, None, None),
        P("row", "col", None, None),
        P("row", "col", None, None, None),
        P(),
        P("row", "col", None),
    )
    out_specs = (P("row", "col", None, None, None), P())
    return jax.shard_map(body, mesh=mesh, in_specs=in_specs, out_specs=out_specs, check_vma=False)
```

```python
import functools

import jax
import jax.numpy as jnp
from jax import lax
from jax.experimental import pallas as pl
from jax.experimental.pallas import tpu as pltpu
from jax.sharding import PartitionSpec as P

BS = 128
WIN = 4
NO = 32
TASKS = 1024
GROUP = 4
UNROLL = 16
NGROUP = 304
ZERO = 64
FIRST, SECOND = 8, 20
SCALE = 1.0 / (32 * 4 * 128) ** 0.5


def swap(value, axis, bit):
    return lax.ppermute(value, axis, [(i, i ^ bit) for i in range(16)])


def pick(stack, index):
    return lax.dynamic_index_in_dim(stack, index, 0, keepdims=False)


def choose(parts, index):
    mask_shape = (WIN,) + (1,) * (parts[0].ndim - 1)
    out = jnp.broadcast_to(parts[0], (WIN,) + parts[0].shape[1:])
    for d in range(1, len(parts)):
        out = jnp.where((index == d).reshape(mask_shape), parts[d], out)
    return out


def scatter_columns(by_x, panels, x):
    parts = [pick(by_x, x)] + [swap(pick(by_x, x ^ d), "col", 4 * d) for d in (1, 2, 3)]
    index = ((x ^ (panels >> 3)) << 1) | (panels & 1)
    return choose([part[None, :, j] for part in parts for j in range(2)], index)


def scatter_rows(by_y, panels, y):
    parts = [pick(by_y, y)] + [swap(pick(by_y, y ^ d), "row", 4 * d) for d in (1, 2, 3)]
    index = ((y ^ (panels >> 3)) << 1) | (panels & 1)
    return choose([part[None, i] for part in parts for i in range(2)], index)


def panels_to_all(own, panels):
    me_r, me_c = lax.axis_index("row"), lax.axis_index("col")
    x, z = me_c >> 2, me_c & 3
    y, zh, core = me_r >> 2, (me_r >> 1) & 1, me_r & 1
    by_q = jnp.moveaxis(own.reshape(2, 2, 4, 2, BS, BS), 2, 0)
    mine = scatter_columns(by_q, panels, x).reshape(WIN, 4, BS, BS)
    by_j = scatter_rows(by_q, panels, y)

    by_z = jnp.moveaxis(mine, 1, 0)
    parts = [pick(by_z, z)] + [swap(pick(by_z, z ^ d), "col", d) for d in (1, 2, 3)]
    held = choose(parts, z ^ ((panels >> 1) & 3))

    by_j = jnp.moveaxis(by_j, 1, 0)
    got = swap(pick(by_j, 1 - core), "row", 1)
    half = choose([pick(by_j, core), got], ((panels >> 1) & 1) ^ core)

    ahead = [swap(held, "col", 4 * d) for d in (1, 2, 3)]
    near = jnp.concatenate([swap(held, "col", d) for d in (1, 2, 3)])
    near, half, *ahead = lax.optimization_barrier((near, half, *ahead))
    behind = [swap(near, "col", 4 * d) for d in (1, 2, 3)]

    half = choose([half, swap(half, "row", 2)], ((panels >> 2) & 1) ^ zh).reshape(WIN * 2, BS, BS)
    half, behind[0] = lax.optimization_barrier((half, behind[0]))
    line = jnp.concatenate([half] + [swap(half, "row", 4 * d) for d in (1, 2, 3)])
    columns = [held, near] + [part for pair in zip(ahead, behind) for part in pair]
    return columns, [line, swap(line, "row", 1)]


def plan(tasks, coords):
    me_r, me_c = lax.axis_index("row"), lax.axis_index("col")
    x, z = me_c >> 2, me_c & 3
    y, core = me_r >> 2, me_r & 1
    outs = tasks[:, 0].reshape(TASKS)
    left = tasks[:, 1].reshape(TASKS)
    right = tasks[:, 2].reshape(TASKS)
    step = jnp.arange(TASKS, dtype=jnp.int32) >> 8
    left = ((x ^ ((left & 7) >> 1)) << 4) + ((z ^ (((left >> 3) << 1) + (left & 1))) << 2) + step
    right = ((core ^ (right >> 3)) << 5) + ((y ^ ((right & 7) >> 1)) << 3) + (step << 1) + (right & 1)
    slots = jnp.arange(NO, dtype=jnp.int32)
    hot = outs[:, None] == slots[None, :]
    hot_bf = hot.astype(jnp.bfloat16)
    ids = jnp.arange(TASKS, dtype=jnp.int32)
    earlier = (ids[None, :] < ids[:, None]).astype(jnp.bfloat16)
    seen = jnp.dot(earlier, hot_bf, preferred_element_type=jnp.float32).astype(jnp.int32)
    counts = jnp.sum(hot.astype(jnp.int32), axis=0)
    groups = (counts + GROUP - 1) >> 2
    diag = coords[0] == coords[1]
    order = jnp.where(diag, 0, NO) + slots
    before = order[None, :] < order[:, None]
    starts = jnp.sum(jnp.where(before, groups[None, :], 0), axis=1)
    rank = jnp.sum(before.astype(jnp.int32), axis=1)
    place = jnp.sum(jnp.where(hot, seen + GROUP * starts[None, :], 0), axis=1)
    place = jnp.where(outs >= 0, place, -1)
    spots = jnp.arange(NGROUP * GROUP, dtype=jnp.int32)
    move = (spots[:, None] == place[None, :]).astype(jnp.bfloat16)
    pair = jnp.stack([left - ZERO, right], axis=1).astype(jnp.bfloat16)
    lists = jnp.dot(move, pair, preferred_element_type=jnp.float32).astype(jnp.int32)
    gid = jnp.arange(NGROUP, dtype=jnp.int32)[:, None]
    target = jnp.sum((gid >= (starts + groups)[None, :]).astype(jnp.int32), axis=1)
    slot_of = jnp.sum(jnp.where(rank[:, None] == slots[None, :], slots[:, None], 0), axis=0)
    limits = jnp.array([0, FIRST, SECOND, NO], jnp.int32)
    bounds = jnp.sum(jnp.where(rank[None, :] < limits[:, None], groups[None, :], 0), axis=1)
    return lists[:, 0] + ZERO, lists[:, 1], target, bounds, slot_of, diag.astype(jnp.int32)


def group_product(left_ref, right_ref, lhs, rhs, group):
    spots = [group * GROUP + k for k in range(GROUP)]
    a = jnp.concatenate([lhs[left_ref[t]] for t in spots], axis=1)
    b = jnp.concatenate([rhs[right_ref[t]] for t in spots], axis=0)
    return jnp.dot(a, b, preferred_element_type=jnp.float32)


def accumulate(part, base, count, left_ref, right_ref, target_ref, bounds_ref, lhs, rhs, acc):
    acc[...] = jnp.zeros_like(acc)
    first, last = bounds_ref[part], bounds_ref[part + 1]

    def some(it, carry):
        for u in range(UNROLL):
            g = first + it * UNROLL + u
            product = group_product(left_ref, right_ref, lhs, rhs, g)
            acc[jnp.minimum(target_ref[g] - base, count)] += product
        return carry

    lax.fori_loop(0, (last - first + UNROLL - 1) >> 4, some, 0)


def first_kernel(left_ref, right_ref, target_ref, bounds_ref, slot_ref, branch_ref, diag_ref, lhs, rhs, own, out, sums, acc, old, new):
    old[...] = jnp.zeros_like(old)
    new[...] = jnp.zeros_like(new)
    accumulate(0, 0, FIRST, left_ref, right_ref, target_ref, bounds_ref, lhs, rhs, acc)

    def finish(i, carry):
        o = slot_ref[i]
        product = acc[i]
        block = own[o].astype(jnp.float32)
        value = jnp.where(branch_ref[o] == 0, product, 2.0 * block - product)
        out[i] = value.astype(jnp.bfloat16)

        @pl.when(diag_ref[o] > 0)
        def _():
            old[...] += block
            new[...] += value

        return carry

    lax.fori_loop(0, FIRST, finish, 0)
    shape = (BS, BS)
    eye = lax.broadcasted_iota(jnp.int32, shape, 0) == lax.broadcasted_iota(jnp.int32, shape, 1)
    sums[...] = jnp.zeros_like(sums)
    sums[0:1, :] = jnp.sum(jnp.where(eye, old[...], 0.0), axis=0, keepdims=True)
    sums[1:2, :] = jnp.sum(jnp.where(eye, new[...], 0.0), axis=0, keepdims=True)


def second_kernel(left_ref, right_ref, target_ref, bounds_ref, slot_ref, branch_ref, lhs, rhs, own, out, acc):
    accumulate(1, FIRST, SECOND - FIRST, left_ref, right_ref, target_ref, bounds_ref, lhs, rhs, acc)

    def finish(i, carry):
        o = slot_ref[FIRST + i]
        product = acc[i]
        value = jnp.where(branch_ref[o] == 0, product, 2.0 * own[o].astype(jnp.float32) - product)
        out[i] = value.astype(jnp.bfloat16)
        return carry

    lax.fori_loop(0, SECOND - FIRST, finish, 0)


def third_kernel(left_ref, right_ref, target_ref, bounds_ref, slot_ref, branch_ref, lhs, rhs, own, first, second, out, acc):
    accumulate(2, SECOND, NO - SECOND, left_ref, right_ref, target_ref, bounds_ref, lhs, rhs, acc)

    def copy_first(i, carry):
        out[slot_ref[i]] = first[i]
        return carry

    def copy_second(i, carry):
        out[slot_ref[FIRST + i]] = second[i]
        return carry

    lax.fori_loop(0, FIRST, copy_first, 0)
    lax.fori_loop(0, SECOND - FIRST, copy_second, 0)

    def finish(i, carry):
        o = slot_ref[SECOND + i]
        product = acc[i]
        value = jnp.where(branch_ref[o] == 0, product, 2.0 * own[o].astype(jnp.float32) - product)
        out[o] = value.astype(jnp.bfloat16)
        return carry

    lax.fori_loop(0, NO - SECOND, finish, 0)


def products(kernel, count, out_shape, scratch, scalars, arrays):
    smem = pl.BlockSpec(memory_space=pltpu.SMEM)
    vmem = pl.BlockSpec(memory_space=pltpu.VMEM)
    return pl.pallas_call(
        kernel,
        out_shape=out_shape,
        in_specs=[smem] * len(scalars) + [vmem] * len(arrays),
        out_specs=jax.tree.map(lambda _: vmem, out_shape),
        scratch_shapes=[pltpu.VMEM((n, BS, BS) if n else (BS, BS), jnp.float32) for n in scratch],
        compiler_params=pltpu.CompilerParams(vmem_limit_bytes=16 << 20),
        cost_estimate=pl.CostEstimate(flops=count << 27, bytes_accessed=8 << 20, transcendentals=0),
        name="block_products",
    )(*scalars, *arrays)


def body(p_blocks, coords, tasks, window_panels, branch):
    own = p_blocks[0, 0]
    left, right, target, bounds, slot_of, diag = plan(tasks[0, 0], coords[0, 0])
    columns, rows = panels_to_all(own, window_panels)
    lhs = jnp.concatenate(columns + [jnp.zeros((1, BS, BS), jnp.bfloat16)])
    arrays = (lhs, jnp.concatenate(rows), own)
    scalars = (left, right, target, bounds, slot_of, branch[0, 0], diag)
    shapes = (jax.ShapeDtypeStruct((FIRST, BS, BS), jnp.bfloat16), jax.ShapeDtypeStruct((8, BS), jnp.float32))
    first, value = products(first_kernel, FIRST, shapes, (FIRST + 1, 0, 0), scalars, arrays)
    for axis, low, high in (("row", 1, 2), ("row", 4, 8), ("col", 1, 2)):
        one, two, three = (swap(value, axis, b) for b in (low, high, low + high))
        value = (value + one) + (two + three)
    scalars = scalars[:6]
    value, own = lax.optimization_barrier((value, own))
    arrays = arrays[:2] + (own,)
    other = swap(value, "col", 4)
    shapes = jax.ShapeDtypeStruct((SECOND - FIRST, BS, BS), jnp.bfloat16)
    second = products(second_kernel, SECOND - FIRST, shapes, (SECOND - FIRST + 1,), scalars, arrays)
    value, second = lax.optimization_barrier((value + other, second))
    other = swap(value, "col", 8)
    shapes = jax.ShapeDtypeStruct((NO, BS, BS), jnp.bfloat16)
    out = products(third_kernel, NO - SECOND, shapes, (NO - SECOND + 1,), scalars, arrays + (first, second))
    traces = jnp.sum(value + other, axis=1)[:2] * SCALE
    return out[None, None], traces


def solution(mesh):
    in_specs = (
        P("row", "col", None, None, None),
        P("row", "col", None, None),
        P("row", "col", None, None, None),
        P(),
        P("row", "col", None),
    )
    out_specs = (P("row", "col", None, None, None), P())
    return jax.shard_map(body, mesh=mesh, in_specs=in_specs, out_specs=out_specs, check_vma=False)
```

```python
import functools

import jax
import jax.numpy as jnp
from jax import lax
from jax.experimental import pallas as pl
from jax.experimental.pallas import tpu as pltpu
from jax.sharding import PartitionSpec as P

BS = 128
WIN = 4
NO = 32
TASKS = 1024
GROUP = 4
UNROLL = 16
NGROUP = 304
ZERO = 64
FIRST, SECOND = 8, 20
SCALE = 1.0 / (32 * 4 * 128) ** 0.5


def swap(value, axis, bit):
    return lax.ppermute(value, axis, [(i, i ^ bit) for i in range(16)])


def pick(stack, index):
    return lax.dynamic_index_in_dim(stack, index, 0, keepdims=False)


def choose(parts, index):
    mask_shape = (WIN,) + (1,) * (parts[0].ndim - 1)
    out = jnp.broadcast_to(parts[0], (WIN,) + parts[0].shape[1:])
    for d in range(1, len(parts)):
        out = jnp.where((index == d).reshape(mask_shape), parts[d], out)
    return out


def scatter_columns(by_x, panels, x):
    parts = [pick(by_x, x)] + [swap(pick(by_x, x ^ d), "col", 4 * d) for d in (1, 2, 3)]
    index = ((x ^ (panels >> 3)) << 1) | (panels & 1)
    return choose([part[None, :, j] for part in parts for j in range(2)], index)


def scatter_rows(by_y, panels, y):
    parts = [pick(by_y, y)] + [swap(pick(by_y, y ^ d), "row", 4 * d) for d in (1, 2, 3)]
    index = ((y ^ (panels >> 3)) << 1) | (panels & 1)
    return choose([part[None, i] for part in parts for i in range(2)], index)


def panels_to_all(own, panels):
    me_r, me_c = lax.axis_index("row"), lax.axis_index("col")
    x, z = me_c >> 2, me_c & 3
    y, zh, core = me_r >> 2, (me_r >> 1) & 1, me_r & 1
    by_q = jnp.moveaxis(own.reshape(2, 2, 4, 2, BS, BS), 2, 0)
    mine = scatter_columns(by_q, panels, x).reshape(WIN, 4, BS, BS)
    by_j = scatter_rows(by_q, panels, y)

    by_z = jnp.moveaxis(mine, 1, 0)
    parts = [pick(by_z, z)] + [swap(pick(by_z, z ^ d), "col", d) for d in (1, 2, 3)]
    held = choose(parts, z ^ ((panels >> 1) & 3))

    by_j = jnp.moveaxis(by_j, 1, 0)
    got = swap(pick(by_j, 1 - core), "row", 1)
    half = choose([pick(by_j, core), got], ((panels >> 1) & 1) ^ core)

    ahead = [swap(held, "col", 4 * d) for d in (1, 2, 3)]
    near = jnp.concatenate([swap(held, "col", d) for d in (1, 2, 3)])
    near, half, *ahead = lax.optimization_barrier((near, half, *ahead))
    behind = [swap(near, "col", 4 * d) for d in (1, 2, 3)]

    half = choose([half, swap(half, "row", 2)], ((panels >> 2) & 1) ^ zh).reshape(WIN * 2, BS, BS)
    half, behind[0] = lax.optimization_barrier((half, behind[0]))
    line = jnp.concatenate([half] + [swap(half, "row", 4 * d) for d in (1, 2, 3)])
    columns = [held, near] + [part for pair in zip(ahead, behind) for part in pair]
    return columns, [line, swap(line, "row", 1)]


def plan(tasks, coords):
    me_r, me_c = lax.axis_index("row"), lax.axis_index("col")
    x, z = me_c >> 2, me_c & 3
    y, core = me_r >> 2, me_r & 1
    outs = tasks[:, 0].reshape(TASKS)
    left = tasks[:, 1].reshape(TASKS)
    right = tasks[:, 2].reshape(TASKS)
    step = jnp.arange(TASKS, dtype=jnp.int32) >> 8
    left = ((x ^ ((left & 7) >> 1)) << 4) + ((z ^ (((left >> 3) << 1) + (left & 1))) << 2) + step
    right = ((core ^ (right >> 3)) << 5) + ((y ^ ((right & 7) >> 1)) << 3) + (step << 1) + (right & 1)
    slots = jnp.arange(NO, dtype=jnp.int32)
    hot = outs[:, None] == slots[None, :]
    hot_bf = hot.astype(jnp.bfloat16)
    ids = jnp.arange(TASKS, dtype=jnp.int32)
    earlier = (ids[None, :] < ids[:, None]).astype(jnp.bfloat16)
    seen = jnp.dot(earlier, hot_bf, preferred_element_type=jnp.float32).astype(jnp.int32)
    counts = jnp.sum(hot.astype(jnp.int32), axis=0)
    groups = (counts + GROUP - 1) >> 2
    diag = coords[0] == coords[1]
    order = jnp.where(diag, 0, NO) + slots
    before = order[None, :] < order[:, None]
    starts = jnp.sum(jnp.where(before, groups[None, :], 0), axis=1)
    rank = jnp.sum(before.astype(jnp.int32), axis=1)
    place = jnp.sum(jnp.where(hot, seen + GROUP * starts[None, :], 0), axis=1)
    place = jnp.where(outs >= 0, place, -1)
    spots = jnp.arange(NGROUP * GROUP, dtype=jnp.int32)
    move = (spots[:, None] == place[None, :]).astype(jnp.bfloat16)
    pair = jnp.stack([left - ZERO, right], axis=1).astype(jnp.bfloat16)
    lists = jnp.dot(move, pair, preferred_element_type=jnp.float32).astype(jnp.int32)
    gid = jnp.arange(NGROUP, dtype=jnp.int32)[:, None]
    target = jnp.sum((gid >= (starts + groups)[None, :]).astype(jnp.int32), axis=1)
    slot_of = jnp.sum(jnp.where(rank[:, None] == slots[None, :], slots[:, None], 0), axis=0)
    limits = jnp.array([0, FIRST, SECOND, NO], jnp.int32)
    bounds = jnp.sum(jnp.where(rank[None, :] < limits[:, None], groups[None, :], 0), axis=1)
    return lists[:, 0] + ZERO, lists[:, 1], target, bounds, slot_of, diag.astype(jnp.int32)


def group_product(left_ref, right_ref, lhs, rhs, group):
    spots = [group * GROUP + k for k in range(GROUP)]
    a = jnp.concatenate([lhs[left_ref[t]] for t in spots], axis=1)
    b = jnp.concatenate([rhs[right_ref[t]] for t in spots], axis=0)
    return jnp.dot(a, b, preferred_element_type=jnp.float32)


def accumulate(part, base, count, left_ref, right_ref, target_ref, bounds_ref, lhs, rhs, acc):
    acc[...] = jnp.zeros_like(acc)
    first, last = bounds_ref[part], bounds_ref[part + 1]

    def some(it, carry):
        for u in range(UNROLL):
            g = first + it * UNROLL + u
            product = group_product(left_ref, right_ref, lhs, rhs, g)
            acc[jnp.minimum(target_ref[g] - base, count)] += product
        return carry

    lax.fori_loop(0, (last - first + UNROLL - 1) >> 4, some, 0)


def first_kernel(left_ref, right_ref, target_ref, bounds_ref, slot_ref, branch_ref, diag_ref, lhs, rhs, own, out, sums, acc, old, new):
    old[...] = jnp.zeros_like(old)
    new[...] = jnp.zeros_like(new)
    accumulate(0, 0, FIRST, left_ref, right_ref, target_ref, bounds_ref, lhs, rhs, acc)

    def finish(i, carry):
        o = slot_ref[i]
        product = acc[i]
        block = own[o].astype(jnp.float32)
        value = jnp.where(branch_ref[o] == 0, product, 2.0 * block - product)
        out[i] = value.astype(jnp.bfloat16)

        @pl.when(diag_ref[o] > 0)
        def _():
            old[...] += block
            new[...] += value

        return carry

    lax.fori_loop(0, FIRST, finish, 0)
    shape = (BS, BS)
    eye = lax.broadcasted_iota(jnp.int32, shape, 0) == lax.broadcasted_iota(jnp.int32, shape, 1)
    sums[...] = jnp.zeros_like(sums)
    sums[0:1, :] = jnp.sum(jnp.where(eye, old[...], 0.0), axis=0, keepdims=True)
    sums[1:2, :] = jnp.sum(jnp.where(eye, new[...], 0.0), axis=0, keepdims=True)


def second_kernel(left_ref, right_ref, target_ref, bounds_ref, slot_ref, branch_ref, lhs, rhs, own, out, acc):
    accumulate(1, FIRST, SECOND - FIRST, left_ref, right_ref, target_ref, bounds_ref, lhs, rhs, acc)

    def finish(i, carry):
        o = slot_ref[FIRST + i]
        product = acc[i]
        value = jnp.where(branch_ref[o] == 0, product, 2.0 * own[o].astype(jnp.float32) - product)
        out[i] = value.astype(jnp.bfloat16)
        return carry

    lax.fori_loop(0, SECOND - FIRST, finish, 0)


def third_kernel(left_ref, right_ref, target_ref, bounds_ref, slot_ref, branch_ref, lhs, rhs, own, first, second, out, acc):
    accumulate(2, SECOND, NO - SECOND, left_ref, right_ref, target_ref, bounds_ref, lhs, rhs, acc)

    def copy_first(i, carry):
        out[slot_ref[i]] = first[i]
        return carry

    def copy_second(i, carry):
        out[slot_ref[FIRST + i]] = second[i]
        return carry

    lax.fori_loop(0, FIRST, copy_first, 0)
    lax.fori_loop(0, SECOND - FIRST, copy_second, 0)

    def finish(i, carry):
        o = slot_ref[SECOND + i]
        product = acc[i]
        value = jnp.where(branch_ref[o] == 0, product, 2.0 * own[o].astype(jnp.float32) - product)
        out[o] = value.astype(jnp.bfloat16)
        return carry

    lax.fori_loop(0, NO - SECOND, finish, 0)


def products(kernel, count, out_shape, scratch, scalars, arrays):
    smem = pl.BlockSpec(memory_space=pltpu.SMEM)
    vmem = pl.BlockSpec(memory_space=pltpu.VMEM)
    return pl.pallas_call(
        kernel,
        out_shape=out_shape,
        in_specs=[smem] * len(scalars) + [vmem] * len(arrays),
        out_specs=jax.tree.map(lambda _: vmem, out_shape),
        scratch_shapes=[pltpu.VMEM((n, BS, BS) if n else (BS, BS), jnp.float32) for n in scratch],
        compiler_params=pltpu.CompilerParams(vmem_limit_bytes=16 << 20),
        cost_estimate=pl.CostEstimate(flops=count << 27, bytes_accessed=8 << 20, transcendentals=0),
        name="block_products",
    )(*scalars, *arrays)


def body(p_blocks, coords, tasks, window_panels, branch):
    own = p_blocks[0, 0]
    left, right, target, bounds, slot_of, diag = plan(tasks[0, 0], coords[0, 0])
    columns, rows = panels_to_all(own, window_panels)
    lhs = jnp.concatenate(columns + [jnp.zeros((1, BS, BS), jnp.bfloat16)])
    arrays = (lhs, jnp.concatenate(rows), own)
    scalars = (left, right, target, bounds, slot_of, branch[0, 0], diag)
    shapes = (jax.ShapeDtypeStruct((FIRST, BS, BS), jnp.bfloat16), jax.ShapeDtypeStruct((8, BS), jnp.float32))
    first, value = products(first_kernel, FIRST, shapes, (FIRST + 1, 0, 0), scalars, arrays)
    for axis, low, high in (("row", 4, 8), ("col", 1, 2), ("col", 4, 8)):
        one, two, three = (swap(value, axis, b) for b in (low, high, low + high))
        value = (value + one) + (two + three)
    scalars = scalars[:6]
    value, own = lax.optimization_barrier((value, own))
    arrays = arrays[:2] + (own,)
    other = swap(value, "row", 1)
    shapes = jax.ShapeDtypeStruct((SECOND - FIRST, BS, BS), jnp.bfloat16)
    second = products(second_kernel, SECOND - FIRST, shapes, (SECOND - FIRST + 1,), scalars, arrays)
    value, second = lax.optimization_barrier((value + other, second))
    other = swap(value, "row", 2)
    shapes = jax.ShapeDtypeStruct((NO, BS, BS), jnp.bfloat16)
    out = products(third_kernel, NO - SECOND, shapes, (NO - SECOND + 1,), scalars, arrays + (first, second))
    traces = jnp.sum(value + other, axis=1)[:2] * SCALE
    return out[None, None], traces


def solution(mesh):
    in_specs = (
        P("row", "col", None, None, None),
        P("row", "col", None, None),
        P("row", "col", None, None, None),
        P(),
        P("row", "col", None),
    )
    out_specs = (P("row", "col", None, None, None), P())
    return jax.shard_map(body, mesh=mesh, in_specs=in_specs, out_specs=out_specs, check_vma=False)
```

```python
import functools

import jax
import jax.numpy as jnp
from jax import lax
from jax.experimental import pallas as pl
from jax.experimental.pallas import tpu as pltpu
from jax.sharding import PartitionSpec as P

BS = 128
WIN = 4
NO = 32
TASKS = 1024
GROUP = 4
UNROLL = 16
NGROUP = 304
ZERO = 64
FIRST, SECOND = 8, 20
SCALE = 1.0 / (32 * 4 * 128) ** 0.5


def swap(value, axis, bit):
    return lax.ppermute(value, axis, [(i, i ^ bit) for i in range(16)])


def pick(stack, index):
    return lax.dynamic_index_in_dim(stack, index, 0, keepdims=False)


def choose(parts, index):
    mask_shape = (WIN,) + (1,) * (parts[0].ndim - 1)
    out = jnp.broadcast_to(parts[0], (WIN,) + parts[0].shape[1:])
    for d in range(1, len(parts)):
        out = jnp.where((index == d).reshape(mask_shape), parts[d], out)
    return out


def scatter_columns(by_x, panels, x):
    parts = [pick(by_x, x)] + [swap(pick(by_x, x ^ d), "col", 4 * d) for d in (1, 2, 3)]
    index = ((x ^ (panels >> 3)) << 1) | (panels & 1)
    return choose([part[None, :, j] for part in parts for j in range(2)], index)


def scatter_rows(by_y, panels, y):
    parts = [pick(by_y, y)] + [swap(pick(by_y, y ^ d), "row", 4 * d) for d in (1, 2, 3)]
    index = ((y ^ (panels >> 3)) << 1) | (panels & 1)
    return choose([part[None, i] for part in parts for i in range(2)], index)


def panels_to_all(own, panels):
    me_r, me_c = lax.axis_index("row"), lax.axis_index("col")
    x, z = me_c >> 2, me_c & 3
    y, zh, core = me_r >> 2, (me_r >> 1) & 1, me_r & 1
    by_q = jnp.moveaxis(own.reshape(2, 2, 4, 2, BS, BS), 2, 0)
    mine = scatter_columns(by_q, panels, x).reshape(WIN, 4, BS, BS)
    by_j = scatter_rows(by_q, panels, y)

    by_z = jnp.moveaxis(mine, 1, 0)
    parts = [pick(by_z, z)] + [swap(pick(by_z, z ^ d), "col", d) for d in (1, 2, 3)]
    held = choose(parts, z ^ ((panels >> 1) & 3))

    by_j = jnp.moveaxis(by_j, 1, 0)
    got = swap(pick(by_j, 1 - core), "row", 1)
    half = choose([pick(by_j, core), got], ((panels >> 1) & 1) ^ core)

    ahead = [swap(held, "col", 4 * d) for d in (1, 2, 3)]
    near = jnp.concatenate([swap(held, "col", d) for d in (1, 2, 3)])
    near, half, *ahead = lax.optimization_barrier((near, half, *ahead))
    behind = [swap(near, "col", 4 * d) for d in (1, 2, 3)]

    half = choose([half, swap(half, "row", 2)], ((panels >> 2) & 1) ^ zh).reshape(WIN * 2, BS, BS)
    half, behind[0] = lax.optimization_barrier((half, behind[0]))
    by_y = [half] + [swap(half, "row", 4 * d) for d in (1, 2, 3)]
    pairs = [jnp.concatenate(by_y[:2]), jnp.concatenate(by_y[2:])]
    columns = [held, near] + [part for pair in zip(ahead, behind) for part in pair]
    return columns, pairs + [swap(pair, "row", 1) for pair in pairs]


def plan(tasks, coords):
    me_r, me_c = lax.axis_index("row"), lax.axis_index("col")
    x, z = me_c >> 2, me_c & 3
    y, core = me_r >> 2, me_r & 1
    outs = tasks[:, 0].reshape(TASKS)
    left = tasks[:, 1].reshape(TASKS)
    right = tasks[:, 2].reshape(TASKS)
    step = jnp.arange(TASKS, dtype=jnp.int32) >> 8
    left = ((x ^ ((left & 7) >> 1)) << 4) + ((z ^ (((left >> 3) << 1) + (left & 1))) << 2) + step
    right = ((core ^ (right >> 3)) << 5) + ((y ^ ((right & 7) >> 1)) << 3) + (step << 1) + (right & 1)
    slots = jnp.arange(NO, dtype=jnp.int32)
    hot = outs[:, None] == slots[None, :]
    hot_bf = hot.astype(jnp.bfloat16)
    ids = jnp.arange(TASKS, dtype=jnp.int32)
    earlier = (ids[None, :] < ids[:, None]).astype(jnp.bfloat16)
    seen = jnp.dot(earlier, hot_bf, preferred_element_type=jnp.float32).astype(jnp.int32)
    counts = jnp.sum(hot.astype(jnp.int32), axis=0)
    groups = (counts + GROUP - 1) >> 2
    diag = coords[0] == coords[1]
    order = jnp.where(diag, 0, NO) + slots
    before = order[None, :] < order[:, None]
    starts = jnp.sum(jnp.where(before, groups[None, :], 0), axis=1)
    rank = jnp.sum(before.astype(jnp.int32), axis=1)
    place = jnp.sum(jnp.where(hot, seen + GROUP * starts[None, :], 0), axis=1)
    place = jnp.where(outs >= 0, place, -1)
    spots = jnp.arange(NGROUP * GROUP, dtype=jnp.int32)
    move = (spots[:, None] == place[None, :]).astype(jnp.bfloat16)
    pair = jnp.stack([left - ZERO, right], axis=1).astype(jnp.bfloat16)
    lists = jnp.dot(move, pair, preferred_element_type=jnp.float32).astype(jnp.int32)
    gid = jnp.arange(NGROUP, dtype=jnp.int32)[:, None]
    target = jnp.sum((gid >= (starts + groups)[None, :]).astype(jnp.int32), axis=1)
    slot_of = jnp.sum(jnp.where(rank[:, None] == slots[None, :], slots[:, None], 0), axis=0)
    limits = jnp.array([0, FIRST, SECOND, NO], jnp.int32)
    bounds = jnp.sum(jnp.where(rank[None, :] < limits[:, None], groups[None, :], 0), axis=1)
    return lists[:, 0] + ZERO, lists[:, 1], target, bounds, slot_of, diag.astype(jnp.int32)


def group_product(left_ref, right_ref, lhs, rhs, group):
    spots = [group * GROUP + k for k in range(GROUP)]
    a = jnp.concatenate([lhs[left_ref[t]] for t in spots], axis=1)
    b = jnp.concatenate([rhs[right_ref[t]] for t in spots], axis=0)
    return jnp.dot(a, b, preferred_element_type=jnp.float32)


def accumulate(part, base, count, left_ref, right_ref, target_ref, bounds_ref, lhs, rhs, acc):
    acc[...] = jnp.zeros_like(acc)
    first, last = bounds_ref[part], bounds_ref[part + 1]

    def some(it, carry):
        for u in range(UNROLL):
            g = first + it * UNROLL + u
            product = group_product(left_ref, right_ref, lhs, rhs, g)
            acc[jnp.minimum(target_ref[g] - base, count)] += product
        return carry

    lax.fori_loop(0, (last - first + UNROLL - 1) >> 4, some, 0)


def first_kernel(left_ref, right_ref, target_ref, bounds_ref, slot_ref, branch_ref, diag_ref, lhs, rhs, own, out, sums, acc, old, new):
    old[...] = jnp.zeros_like(old)
    new[...] = jnp.zeros_like(new)
    accumulate(0, 0, FIRST, left_ref, right_ref, target_ref, bounds_ref, lhs, rhs, acc)

    def finish(i, carry):
        o = slot_ref[i]
        product = acc[i]
        block = own[o].astype(jnp.float32)
        value = jnp.where(branch_ref[o] == 0, product, 2.0 * block - product)
        out[i] = value.astype(jnp.bfloat16)

        @pl.when(diag_ref[o] > 0)
        def _():
            old[...] += block
            new[...] += value

        return carry

    lax.fori_loop(0, FIRST, finish, 0)
    shape = (BS, BS)
    eye = lax.broadcasted_iota(jnp.int32, shape, 0) == lax.broadcasted_iota(jnp.int32, shape, 1)
    sums[...] = jnp.zeros_like(sums)
    sums[0:1, :] = jnp.sum(jnp.where(eye, old[...], 0.0), axis=0, keepdims=True)
    sums[1:2, :] = jnp.sum(jnp.where(eye, new[...], 0.0), axis=0, keepdims=True)


def second_kernel(left_ref, right_ref, target_ref, bounds_ref, slot_ref, branch_ref, lhs, rhs, own, out, acc):
    accumulate(1, FIRST, SECOND - FIRST, left_ref, right_ref, target_ref, bounds_ref, lhs, rhs, acc)

    def finish(i, carry):
        o = slot_ref[FIRST + i]
        product = acc[i]
        value = jnp.where(branch_ref[o] == 0, product, 2.0 * own[o].astype(jnp.float32) - product)
        out[i] = value.astype(jnp.bfloat16)
        return carry

    lax.fori_loop(0, SECOND - FIRST, finish, 0)


def third_kernel(left_ref, right_ref, target_ref, bounds_ref, slot_ref, branch_ref, lhs, rhs, own, first, second, out, acc):
    accumulate(2, SECOND, NO - SECOND, left_ref, right_ref, target_ref, bounds_ref, lhs, rhs, acc)

    def copy_first(i, carry):
        out[slot_ref[i]] = first[i]
        return carry

    def copy_second(i, carry):
        out[slot_ref[FIRST + i]] = second[i]
        return carry

    lax.fori_loop(0, FIRST, copy_first, 0)
    lax.fori_loop(0, SECOND - FIRST, copy_second, 0)

    def finish(i, carry):
        o = slot_ref[SECOND + i]
        product = acc[i]
        value = jnp.where(branch_ref[o] == 0, product, 2.0 * own[o].astype(jnp.float32) - product)
        out[o] = value.astype(jnp.bfloat16)
        return carry

    lax.fori_loop(0, NO - SECOND, finish, 0)


def products(kernel, count, out_shape, scratch, scalars, arrays):
    smem = pl.BlockSpec(memory_space=pltpu.SMEM)
    vmem = pl.BlockSpec(memory_space=pltpu.VMEM)
    return pl.pallas_call(
        kernel,
        out_shape=out_shape,
        in_specs=[smem] * len(scalars) + [vmem] * len(arrays),
        out_specs=jax.tree.map(lambda _: vmem, out_shape),
        scratch_shapes=[pltpu.VMEM((n, BS, BS) if n else (BS, BS), jnp.float32) for n in scratch],
        compiler_params=pltpu.CompilerParams(vmem_limit_bytes=16 << 20),
        cost_estimate=pl.CostEstimate(flops=count << 27, bytes_accessed=8 << 20, transcendentals=0),
        name="block_products",
    )(*scalars, *arrays)


def body(p_blocks, coords, tasks, window_panels, branch):
    own = p_blocks[0, 0]
    left, right, target, bounds, slot_of, diag = plan(tasks[0, 0], coords[0, 0])
    columns, rows = panels_to_all(own, window_panels)
    lhs = jnp.concatenate(columns + [jnp.zeros((1, BS, BS), jnp.bfloat16)])
    arrays = (lhs, jnp.concatenate(rows), own)
    scalars = (left, right, target, bounds, slot_of, branch[0, 0], diag)
    shapes = (jax.ShapeDtypeStruct((FIRST, BS, BS), jnp.bfloat16), jax.ShapeDtypeStruct((8, BS), jnp.float32))
    first, value = products(first_kernel, FIRST, shapes, (FIRST + 1, 0, 0), scalars, arrays)
    for axis, low, high in (("row", 4, 8), ("col", 1, 2), ("col", 4, 8)):
        one, two, three = (swap(value, axis, b) for b in (low, high, low + high))
        value = (value + one) + (two + three)
    scalars = scalars[:6]
    value, own = lax.optimization_barrier((value, own))
    arrays = arrays[:2] + (own,)
    other = swap(value, "row", 1)
    shapes = jax.ShapeDtypeStruct((SECOND - FIRST, BS, BS), jnp.bfloat16)
    second = products(second_kernel, SECOND - FIRST, shapes, (SECOND - FIRST + 1,), scalars, arrays)
    value, second = lax.optimization_barrier((value + other, second))
    other = swap(value, "row", 2)
    shapes = jax.ShapeDtypeStruct((NO, BS, BS), jnp.bfloat16)
    out = products(third_kernel, NO - SECOND, shapes, (NO - SECOND + 1,), scalars, arrays + (first, second))
    traces = jnp.sum(value + other, axis=1)[:2] * SCALE
    return out[None, None], traces


def solution(mesh):
    in_specs = (
        P("row", "col", None, None, None),
        P("row", "col", None, None),
        P("row", "col", None, None, None),
        P(),
        P("row", "col", None),
    )
    out_specs = (P("row", "col", None, None, None), P())
    return jax.shard_map(body, mesh=mesh, in_specs=in_specs, out_specs=out_specs, check_vma=False)
```
